32 devices in a mesh: samp: 2 (over x), gene: 4 (over z), snp: 4 (over y, core).
Axes of the slice: x: 2, y: 2, z: 4, core: 2. Of those that a mesh axis runs over, the one named last changes fastest.
Arguments:
- expression: bfloat16 [512, 2048], P('samp', ('gene', 'snp')), may hold values from -6 to 6
- loadings: bfloat16 [2048, 128], P(('gene', 'snp')), may hold values from -0.125 to 0.125
- dosage: bfloat16 [512, 16384], P(None, ('gene', 'snp')), may hold values from 0 to 2
Outputs:
- assoc: bfloat16 [16, 2, 64, 16384], P(None, 'samp', None, ('gene', 'snp'))
The draws below stay inside these ranges and needn't reach their ends.
All inputs are finite; a program needn't handle non-finite values.
Results may differ from the reference program's by a relative error of at most 0.0065.
Values may be sent and summed in bfloat16 or wider, within the bound.
A program may use at most 64 MiB of HBM per device.

```python
import jax
import jax.numpy as jnp
from jax import lax

K = 128
GP = 64
S = 512
BLOCKS = 16
G_LOC = 128
G = 2048
P_SIZE = 16384
N_SAMP = 2


def shard_levels(own_key, shape, pieces, low, high):
    gain, own = 1.0, jax.random.fold_in(own_key, 6)
    for axis_at, shards_of in pieces:
        steps = jnp.exp(jax.random.uniform(jax.random.fold_in(own, axis_at), (shards_of,), jnp.float32, low / len(pieces), high / len(pieces)))
        gain = gain * jnp.repeat(steps, shape[axis_at] // shards_of).reshape([-1 if axis == axis_at else 1 for axis in range(len(shape))])
    return gain


def bell_draw(rng, dims, deviation, most, pieces=(), kind=jnp.bfloat16):
    factor_of = shard_levels(rng, dims, pieces, -0.22, 0.18) if pieces else 1.0
    drawn = jax.random.normal(rng, dims, jnp.float32) * deviation * factor_of
    return jnp.minimum(jnp.maximum(drawn, -most), most).astype(kind)


def setup_inputs(seed: int = 0) -> dict:
    arg_keys = jax.random.split(jax.random.key(seed), 4)
    return {
        "expression": bell_draw(arg_keys[0], (S, G), 1.0, 6.0, ((0, 2), (1, 16))),
        "loadings": bell_draw(arg_keys[1], (G, K), G ** -0.5, 0.125, ((0, 16),)),
        "dosage": jnp.clip(2.0 * jax.random.uniform(arg_keys[2], (S, P_SIZE), jnp.float32) ** shard_levels(arg_keys[2], (S, P_SIZE), ((1, 16),), -0.2, 0.2), 0.0, 2.0).astype(jnp.bfloat16),
    }


ridge_factor = 1.0
ridge_sample = 1.0

def reference(expression, loadings, dosage):
    contract = (((0,), (0,)), ((), ()))
    identity = jnp.eye(K, dtype=jnp.float32)
    factor_sum = jnp.dot(expression.astype(jnp.float32), loadings.astype(jnp.float32), preferred_element_type=jnp.float32)
    gram = lax.dot_general(loadings.astype(jnp.float32), loadings.astype(jnp.float32), contract, preferred_element_type=jnp.float32) + ridge_factor * identity
    lower_gram = jnp.linalg.cholesky(gram)
    factors = jax.scipy.linalg.cho_solve((lower_gram, True), factor_sum.T).T.astype(jnp.bfloat16)
    hessian = lax.dot_general(factors.astype(jnp.float32), factors.astype(jnp.float32), contract, preferred_element_type=jnp.float32) + ridge_sample * identity
    cross = lax.dot_general(factors.astype(jnp.float32), expression.astype(jnp.float32), contract, preferred_element_type=jnp.float32)
    lower_hess = jnp.linalg.cholesky(hessian)
    fit_coef = jax.scipy.linalg.cho_solve((lower_hess, True), cross).astype(jnp.bfloat16)
    fitted = lax.dot_general(fit_coef.astype(jnp.float32), factors.astype(jnp.float32), (((0,), (1,)), ((), ())), preferred_element_type=jnp.float32)
    residual_t = (expression.T.astype(jnp.float32) - fitted).astype(jnp.bfloat16)
    norm_scale = 1.0 / jnp.sqrt(jnp.float32(S))
    gene_blocks = residual_t.reshape(BLOCKS, G_LOC, S)

    def block_scores(block_rows):
        return (jnp.dot(block_rows.astype(jnp.float32), dosage.astype(jnp.float32), preferred_element_type=jnp.float32) * norm_scale).astype(jnp.bfloat16)
    scores = lax.map(block_scores, gene_blocks)
    return scores.reshape(BLOCKS, N_SAMP, GP, P_SIZE)
```

```python
import functools

import jax
import jax.numpy as jnp
from jax import lax
from jax.experimental import pallas as pl
from jax.experimental.pallas import tpu as pltpu
from jax.sharding import PartitionSpec as P

ridge_factor = 1.0
ridge_sample = 1.0
MESH = pl.DeviceIdType.MESH
VMEM_LIMIT = 56 * 1024 * 1024


def eye(n, value):
    rows = lax.broadcasted_iota(jnp.int32, (n, n), 0)
    cols = lax.broadcasted_iota(jnp.int32, (n, n), 1)
    return jnp.where(rows == cols, jnp.float32(value), jnp.float32(0.0))


def spd_inverse(a):
    n = a.shape[0]
    lane_top = lax.broadcasted_iota(jnp.int32, (8, n), 1)
    sub_top = lax.broadcasted_iota(jnp.int32, (8, n), 0)
    lane_rest = lax.broadcasted_iota(jnp.int32, (n - 8, n), 1)

    def round_of_pivots(_, a):
        top, rest = a[:8], a[8:]
        for k in range(8):
            row = top[k : k + 1, :]
            inv = 1.0 / row[:, k : k + 1]
            scaled = jnp.where(lane_top[:1] == k, inv, row * inv)
            top_col = jnp.where(sub_top == k, -1.0, jnp.broadcast_to(top[:, k : k + 1], (8, n)))
            rest_col = rest[:, k : k + 1]
            top = jnp.where((sub_top == k) | (lane_top == k), 0.0, top) - top_col * scaled
            rest = jnp.where(lane_rest == k, 0.0, rest) - rest_col * scaled
        return pltpu.roll(jnp.concatenate([rest, top], axis=0), n - 8, 1)

    return lax.fori_loop(0, n // 8, round_of_pivots, a)


def halves(x):
    high = x.astype(jnp.bfloat16)
    low = (x - high.astype(jnp.float32)).astype(jnp.bfloat16)
    return high, low


def factor_kernel(
    sizes, expr_ref, load_ref, panel_ref, fac_ref, proj_ref,
    part, got, own, gram_all, sum_all, expr_t,
    rs_send, rs_recv, ag_send, ag_recv, gram_send, gram_recv, x_send, x_recv, pan_send, pan_recv,
):
    ns, ng, np_ = sizes
    nb = ng * np_
    total = ns * nb
    nl = 2 if np_ % 2 == 0 else 1
    nh = np_ // nl
    s_loc = expr_ref.shape[0]
    k = load_ref.shape[1]
    gp = expr_ref.shape[1] // ns
    rows_f, rows_g = s_loc // nb, k // nb
    s, g, p = lax.axis_index("samp"), lax.axis_index("gene"), lax.axis_index("snp")
    b = g * np_ + p
    q = s * nb + b
    hi, lo = p // nl, p % nl

    def place(q_):
        s_, b_ = q_ // nb, q_ % nb
        return (s_, b_ // np_, b_ % np_), s_, b_

    barrier = pltpu.get_barrier_semaphore()

    def greet(j, c):
        dev, _, _ = place(lax.rem(q + j, total))
        pl.semaphore_signal(barrier, inc=1, device_id=dev, device_id_type=MESH)
        return c

    lax.fori_loop(1, total, greet, 0)

    expr = expr_ref[...]
    load = load_ref[...]
    fac_part = jnp.dot(expr, load, preferred_element_type=jnp.float32)
    part[:, :rows_f, :] = fac_part.reshape(nb, rows_f, k)
    gram_part = lax.dot_general(load, load, (((0,), (0,)), ((), ())), preferred_element_type=jnp.float32)
    part[:, rows_f:, :] = gram_part.reshape(nb, rows_g, k)
    expr_t[...] = expr.T

    pl.semaphore_wait(barrier, total - 1)

    def rs_copy(j):
        peer = lax.rem(b + j, nb)
        return pltpu.make_async_remote_copy(
            src_ref=part.at[peer], dst_ref=got.at[j],
            send_sem=rs_send.at[j], recv_sem=rs_recv.at[j],
            device_id=(s, peer // np_, peer % np_), device_id_type=MESH,
        )

    def x_copy(i, arriving=False):
        peer = lax.rem(s + i, ns)
        source = lax.rem(s - i + ns, ns) if arriving else s
        return pltpu.make_async_remote_copy(
            src_ref=expr_t.at[pl.ds(pl.multiple_of(peer * gp, gp), gp), :],
            dst_ref=panel_ref.at[b, :, pl.ds(pl.multiple_of(source * s_loc, s_loc), s_loc)],
            send_sem=x_send.at[i], recv_sem=x_recv.at[i],
            device_id=(peer, g, p), device_id_type=MESH,
        )

    def loop(lo_, hi_, fn):
        def step(i, c):
            fn(i)
            return c

        lax.fori_loop(lo_, hi_, step, 0)

    loop(1, nb, lambda j: rs_copy(j).start())
    loop(1, ns, lambda i: x_copy(i).start())
    panel_ref[b, :, pl.ds(pl.multiple_of(s * s_loc, s_loc), s_loc)] = expr_t[
        pl.ds(pl.multiple_of(s * gp, gp), gp), :
    ]

    loop(1, nb, lambda j: rs_copy(j).wait_recv())
    acc = part[b]
    for j in range(1, nb):
        acc = acc + got[j]
    own[...] = acc

    def gram_copy(j, arriving=False):
        peer = lax.rem(b + j, nb)
        source = lax.rem(b - j + nb, nb) if arriving else b
        return pltpu.make_async_remote_copy(
            src_ref=own.at[pl.ds(rows_f, rows_g), :],
            dst_ref=gram_all.at[pl.ds(pl.multiple_of(source * rows_g, rows_g), rows_g), :],
            send_sem=gram_send.at[j], recv_sem=gram_recv.at[j],
            device_id=(s, peer // np_, peer % np_), device_id_type=MESH,
        )

    def sum_copy(j, arriving=False):
        dev, _, _ = place(lax.rem(q + j, total))
        source = lax.rem(q - j + total, total) if arriving else q
        return pltpu.make_async_remote_copy(
            src_ref=own.at[pl.ds(0, rows_f), :],
            dst_ref=sum_all.at[pl.ds(pl.multiple_of(source * rows_f, rows_f), rows_f), :],
            send_sem=ag_send.at[j], recv_sem=ag_recv.at[j],
            device_id=dev, device_id_type=MESH,
        )

    loop(1, nb, lambda j: gram_copy(j).start())
    loop(1, total, lambda j: sum_copy(j).start())
    gram_all[pl.ds(pl.multiple_of(b * rows_g, rows_g), rows_g), :] = acc[rows_f:]
    sum_all[pl.ds(pl.multiple_of(q * rows_f, rows_f), rows_f), :] = acc[:rows_f]

    def pan_copy(slot, block, dev):
        return pltpu.make_async_remote_copy(
            src_ref=panel_ref.at[block], dst_ref=panel_ref.at[block],
            send_sem=pan_send.at[slot], recv_sem=pan_recv.at[block],
            device_id=dev, device_id_type=MESH,
        )

    def gene_send(i):
        return pan_copy(i, b, (s, lax.rem(g + i, ng), p))

    def high_send(i):
        h, g_ = 1 + i // ng, i % ng
        return pan_copy(ng + i, g_ * np_ + p, (s, g, lax.rem(hi + h, nh) * nl + lo))

    def low_send(i):
        g_, h = i // nh, i % nh
        return pan_copy(
            ng + ng * (nh - 1) + i, g_ * np_ + h * nl + lo, (s, g, hi * nl + lax.rem(lo + 1, nl))
        )

    n_high = ng * (nh - 1)
    n_low = nb // nl if nl > 1 else 0

    loop(1, ns, lambda i: x_copy(i, True).wait_recv())
    loop(1, ng, lambda i: gene_send(i).start())

    loop(1, nb, lambda j: gram_copy(j, True).wait_recv())
    gram_inv = spd_inverse(gram_all[...] + eye(k, ridge_factor))

    me = (s, g, p)
    loop(1, ng, lambda i: pan_copy(0, lax.rem(g + i, ng) * np_ + p, me).wait_recv())
    loop(0, n_high, lambda i: high_send(i).start())

    loop(1, total, lambda j: sum_copy(j, True).wait_recv())
    factors = jnp.dot(
        sum_all[...], gram_inv, preferred_element_type=jnp.float32, precision=lax.Precision.HIGHEST
    ).astype(jnp.bfloat16)
    fac_ref[...] = factors
    hess = lax.dot_general(
        factors, factors, (((0,), (0,)), ((), ())), preferred_element_type=jnp.float32
    )
    hess_inv = spd_inverse(hess + eye(k, ridge_sample))

    def high_wait(i):
        h, g_ = 1 + i // ng, i % ng
        pan_copy(0, g_ * np_ + lax.rem(hi + h, nh) * nl + lo, me).wait_recv()

    loop(0, n_high, high_wait)
    loop(0, n_low, lambda i: low_send(i).start())

    inv_high, inv_low = halves(hess_inv)
    proj = jnp.dot(factors, inv_high, preferred_element_type=jnp.float32) + jnp.dot(
        factors, inv_low, preferred_element_type=jnp.float32
    )
    proj_high, proj_low = halves(proj)
    proj_ref[:, :k] = proj_high
    proj_ref[:, k:] = proj_low

    def low_wait(i):
        g_, h = i // nh, i % nh
        pan_copy(0, g_ * np_ + h * nl + lax.rem(lo + 1, nl), me).wait_recv()

    loop(0, n_low, low_wait)

    loop(1, nb, lambda j: rs_copy(j).wait_send())
    loop(1, ns, lambda i: x_copy(i).wait_send())
    loop(1, nb, lambda j: gram_copy(j).wait_send())
    loop(1, total, lambda j: sum_copy(j).wait_send())
    loop(1, ng, lambda i: gene_send(i).wait_send())
    loop(0, n_high, lambda i: high_send(i).wait_send())
    loop(0, n_low, lambda i: low_send(i).wait_send())


def assoc_kernel(norm_scale, panel_ref, proj_ref, fac_ref, dosage_ref, out_ref):
    panel = panel_ref[...]
    k = fac_ref.shape[1]
    both = jnp.dot(panel, proj_ref[...], preferred_element_type=jnp.float32)
    coef = (both[:, :k] + both[:, k:]).astype(jnp.bfloat16)
    fitted = lax.dot_general(
        coef, fac_ref[...], (((1,), (1,)), ((), ())), preferred_element_type=jnp.float32
    )
    residual = (panel.astype(jnp.float32) - fitted).astype(jnp.bfloat16)
    totals = jnp.dot(residual, dosage_ref[...], preferred_element_type=jnp.float32)
    out_ref[...] = (totals * norm_scale).astype(jnp.bfloat16)


def body(expression, loadings, dosage):
    ns, ng, np_ = lax.axis_size("samp"), lax.axis_size("gene"), lax.axis_size("snp")
    nb = ng * np_
    total = ns * nb
    s_loc, g_loc = expression.shape
    k = loadings.shape[1]
    gp = g_loc // ns
    samples, snps = dosage.shape
    rows_f, rows_g = s_loc // nb, k // nb
    f32, bf16 = jnp.float32, jnp.bfloat16
    dma = pltpu.SemaphoreType.DMA
    vmem = pl.BlockSpec(memory_space=pltpu.VMEM)
    n_pan = ng + np_ * ng + nb
    panels, factors, proj = pl.pallas_call(
        functools.partial(factor_kernel, (ns, ng, np_)),
        out_shape=(
            jax.ShapeDtypeStruct((nb, gp, samples), bf16),
            jax.ShapeDtypeStruct((samples, k), bf16),
            jax.ShapeDtypeStruct((samples, 2 * k), bf16),
        ),
        in_specs=[vmem, vmem],
        out_specs=(vmem, vmem, vmem),
        scratch_shapes=[
            pltpu.VMEM((nb, rows_f + rows_g, k), f32),
            pltpu.VMEM((nb, rows_f + rows_g, k), f32),
            pltpu.VMEM((rows_f + rows_g, k), f32),
            pltpu.VMEM((k, k), f32),
            pltpu.VMEM((samples, k), f32),
            pltpu.VMEM((g_loc, s_loc), bf16),
            dma((nb,)), dma((nb,)), dma((total,)), dma((total,)), dma((nb,)), dma((nb,)),
            dma((ns,)), dma((ns,)), dma((n_pan,)), dma((nb,)),
        ],
        compiler_params=pltpu.CompilerParams(
            collective_id=0, has_side_effects=True, vmem_limit_bytes=VMEM_LIMIT
        ),
        name="factor_exchange",
    )(expression, loadings)
    rows = min(4 * gp, nb * gp)
    const = lambda i: (0, 0)
    out = pl.pallas_call(
        functools.partial(assoc_kernel, 1.0 / samples**0.5),
        grid=(nb * gp // rows,),
        out_shape=jax.ShapeDtypeStruct((nb * gp, snps), bf16),
        in_specs=[
            pl.BlockSpec((rows, samples), lambda i: (i, 0)),
            pl.BlockSpec((samples, 2 * k), const),
            pl.BlockSpec((samples, k), const),
            pl.BlockSpec((samples, snps), const),
        ],
        out_specs=pl.BlockSpec((rows, snps), lambda i: (i, 0)),
        compiler_params=pltpu.CompilerParams(vmem_limit_bytes=VMEM_LIMIT),
        name="association",
    )(panels.reshape(nb * gp, samples), proj, factors, dosage)
    return out.reshape(nb, 1, gp, snps)


def solution(mesh):
    placed = (P("samp", ("gene", "snp")), P(("gene", "snp"), None), P(None, ("gene", "snp")))
    return jax.shard_map(
        body,
        mesh=mesh,
        in_specs=placed,
        out_specs=P(None, "samp", None, ("gene", "snp")),
        check_vma=False,
    )
```

```python
import functools

import jax
import jax.numpy as jnp
from jax import lax
from jax.experimental import pallas as pl
from jax.experimental.pallas import tpu as pltpu
from jax.sharding import PartitionSpec as P

ridge_factor = 1.0
ridge_sample = 1.0
MESH = pl.DeviceIdType.MESH
MIB = 1024 * 1024


def eye(n, value):
    rows = lax.broadcasted_iota(jnp.int32, (n, n), 0)
    cols = lax.broadcasted_iota(jnp.int32, (n, n), 1)
    return jnp.where(rows == cols, jnp.float32(value), jnp.float32(0.0))


def reciprocal(d):
    guess = pltpu.reciprocal(d, approx=True)
    return guess * (2.0 - d * guess)


def sweep_block(rows, i):
    n = rows[0].shape[1]
    at = 8 * i
    lane = lax.broadcasted_iota(jnp.int32, (8, n), 1)
    sub = lax.broadcasted_iota(jnp.int32, (8, n), 0)

    def full(x):
        return jnp.broadcast_to(x, (8, n))

    top = rows[i]
    cols = [full(top[:, at + j : at + j + 1]) for j in range(8)]
    for k in range(8):
        on = sub == k
        col = cols[k]
        inv = reciprocal(full(col[k : k + 1]))
        top = jnp.where(lane == at + k, jnp.where(on, 1.0, 0.0), top)
        pivot_row = full(top[k : k + 1]) * inv
        top = jnp.where(on, pivot_row, top - col * pivot_row)
        for j in range(k + 1, 8):
            pivot_col = full(cols[j][k : k + 1]) * inv
            cols[j] = jnp.where(on, pivot_col, cols[j] - col * pivot_col)
    weights = [full(top[j : j + 1]) for j in range(8)]
    in_block = (lane >= at) & (lane < at + 8)
    out = []
    for r, x in enumerate(rows):
        if r == i:
            out.append(top)
            continue
        even = full(x[:, at : at + 1]) * weights[0]
        odd = full(x[:, at + 1 : at + 2]) * weights[1]
        for j in range(2, 8, 2):
            even = even + full(x[:, at + j : at + j + 1]) * weights[j]
            odd = odd + full(x[:, at + j + 1 : at + j + 2]) * weights[j + 1]
        out.append(jnp.where(in_block, 0.0, x) - (even + odd))
    return out


def spd_inverse(a):
    n = a.shape[0]
    rows = [a[8 * i : 8 * i + 8] for i in range(n // 8)]
    for i in range(n // 8):
        rows = sweep_block(rows, i)
    return jnp.concatenate(rows, axis=0)


def halves(x):
    high = x.astype(jnp.bfloat16)
    low = (x - high.astype(jnp.float32)).astype(jnp.bfloat16)
    return high, low


def factor_kernel(
    sizes, expr_ref, load_ref, dosage_ref, panel_ref, fac_ref, proj_ref, near_ref,
    part, got, own, gram_all, sum_all, expr_t, expr_in, load_in,
    rs_send, rs_recv, ag_send, ag_recv, gram_send, gram_recv, x_send, x_recv, pan_send, pan_recv, near_sem, in_sem,
):
    ns, ng, np_ = sizes
    nb = ng * np_
    total = ns * nb
    nl = 2 if np_ % 2 == 0 else 1
    nh = np_ // nl
    s_loc = expr_ref.shape[0]
    k = load_ref.shape[1]
    gp = expr_ref.shape[1] // ns
    rows_f, rows_g = s_loc // nb, k // nb
    s, g, p = lax.axis_index("samp"), lax.axis_index("gene"), lax.axis_index("snp")
    b = g * np_ + p
    q = s * nb + b
    hi, lo = p // nl, p % nl

    def place(q_):
        s_, b_ = q_ // nb, q_ % nb
        return (s_, b_ // np_, b_ % np_), s_, b_

    staged = (
        pltpu.make_async_copy(expr_ref, expr_in, in_sem.at[0]),
        pltpu.make_async_copy(load_ref, load_in, in_sem.at[1]),
    )
    for copy in staged:
        copy.start()
    barrier = pltpu.get_barrier_semaphore()

    def greet(j, c):
        dev, _, _ = place(lax.rem(q + j, total))
        pl.semaphore_signal(barrier, inc=1, device_id=dev, device_id_type=MESH)
        return c

    lax.fori_loop(1, total, greet, 0)

    near = pltpu.make_async_copy(dosage_ref, near_ref, near_sem)
    near.start()
    for copy in staged:
        copy.wait()
    expr = expr_in[...]
    load = load_in[...]
    fac_part = jnp.dot(expr, load, preferred_element_type=jnp.float32)
    part[:, :rows_f, :] = fac_part.reshape(nb, rows_f, k)
    gram_part = lax.dot_general(load, load, (((0,), (0,)), ((), ())), preferred_element_type=jnp.float32)
    part[:, rows_f:, :] = gram_part.reshape(nb, rows_g, k)
    expr_t[...] = expr.T

    pl.semaphore_wait(barrier, total - 1)

    def rs_copy(j):
        peer = lax.rem(b + j, nb)
        return pltpu.make_async_remote_copy(
            src_ref=part.at[peer], dst_ref=got.at[j],
            send_sem=rs_send.at[j], recv_sem=rs_recv.at[j],
            device_id=(s, peer // np_, peer % np_), device_id_type=MESH,
        )

    def x_copy(i, arriving=False):
        peer = lax.rem(s + i, ns)
        source = lax.rem(s - i + ns, ns) if arriving else s
        return pltpu.make_async_remote_copy(
            src_ref=expr_t.at[pl.ds(pl.multiple_of(peer * gp, gp), gp), :],
            dst_ref=panel_ref.at[b, :, pl.ds(pl.multiple_of(source * s_loc, s_loc), s_loc)],
            send_sem=x_send.at[i], recv_sem=x_recv.at[i],
            device_id=(peer, g, p), device_id_type=MESH,
        )

    def loop(lo_, hi_, fn):
        def step(i, c):
            fn(i)
            return c

        lax.fori_loop(lo_, hi_, step, 0)

    loop(1, nb, lambda j: rs_copy(j).start())
    loop(1, ns, lambda i: x_copy(i).start())
    panel_ref[b, :, pl.ds(pl.multiple_of(s * s_loc, s_loc), s_loc)] = expr_t[
        pl.ds(pl.multiple_of(s * gp, gp), gp), :
    ]

    loop(1, nb, lambda j: rs_copy(j).wait_recv())
    acc = part[b]
    for j in range(1, nb):
        acc = acc + got[j]
    own[...] = acc

    def gram_copy(j, arriving=False):
        peer = lax.rem(b + j, nb)
        source = lax.rem(b - j + nb, nb) if arriving else b
        return pltpu.make_async_remote_copy(
            src_ref=own.at[pl.ds(rows_f, rows_g), :],
            dst_ref=gram_all.at[pl.ds(pl.multiple_of(source * rows_g, rows_g), rows_g), :],
            send_sem=gram_send.at[j], recv_sem=gram_recv.at[j],
            device_id=(s, peer // np_, peer % np_), device_id_type=MESH,
        )

    def sum_copy(j, arriving=False):
        dev, _, _ = place(lax.rem(q + j, total))
        source = lax.rem(q - j + total, total) if arriving else q
        return pltpu.make_async_remote_copy(
            src_ref=own.at[pl.ds(0, rows_f), :],
            dst_ref=sum_all.at[pl.ds(pl.multiple_of(source * rows_f, rows_f), rows_f), :],
            send_sem=ag_send.at[j], recv_sem=ag_recv.at[j],
            device_id=dev, device_id_type=MESH,
        )

    loop(1, nb, lambda j: gram_copy(j).start())
    loop(1, total, lambda j: sum_copy(j).start())
    gram_all[pl.ds(pl.multiple_of(b * rows_g, rows_g), rows_g), :] = acc[rows_f:]
    sum_all[pl.ds(pl.multiple_of(q * rows_f, rows_f), rows_f), :] = acc[:rows_f]

    def pan_copy(slot, block, dev):
        return pltpu.make_async_remote_copy(
            src_ref=panel_ref.at[block], dst_ref=panel_ref.at[block],
            send_sem=pan_send.at[slot], recv_sem=pan_recv.at[block],
            device_id=dev, device_id_type=MESH,
        )

    def gene_send(i):
        return pan_copy(i, b, (s, lax.rem(g + i, ng), p))

    def high_send(i):
        h, g_ = 1 + i // ng, i % ng
        return pan_copy(ng + i, g_ * np_ + p, (s, g, lax.rem(hi + h, nh) * nl + lo))

    def low_send(i):
        g_, h = i // nh, i % nh
        return pan_copy(
            ng + ng * (nh - 1) + i, g_ * np_ + h * nl + lo, (s, g, hi * nl + lax.rem(lo + 1, nl))
        )

    n_high = ng * (nh - 1)
    n_low = nb // nl if nl > 1 else 0

    loop(1, ns, lambda i: x_copy(i, True).wait_recv())
    loop(1, ng, lambda i: gene_send(i).start())

    loop(1, nb, lambda j: gram_copy(j, True).wait_recv())
    gram_inv = spd_inverse(gram_all[...] + eye(k, ridge_factor))

    me = (s, g, p)
    loop(1, ng, lambda i: pan_copy(0, lax.rem(g + i, ng) * np_ + p, me).wait_recv())
    loop(0, n_high, lambda i: high_send(i).start())

    loop(1, total, lambda j: sum_copy(j, True).wait_recv())
    factors = jnp.dot(
        sum_all[...], gram_inv, preferred_element_type=jnp.float32, precision=lax.Precision.HIGHEST
    ).astype(jnp.bfloat16)
    fac_ref[...] = factors
    hess = lax.dot_general(
        factors, factors, (((0,), (0,)), ((), ())), preferred_element_type=jnp.float32
    )
    hess_inv = spd_inverse(hess + eye(k, ridge_sample))

    def high_wait(i):
        h, g_ = 1 + i // ng, i % ng
        pan_copy(0, g_ * np_ + lax.rem(hi + h, nh) * nl + lo, me).wait_recv()

    loop(0, n_high, high_wait)
    loop(0, n_low, lambda i: low_send(i).start())

    inv_high, inv_low = halves(hess_inv)
    proj = jnp.dot(factors, inv_high, preferred_element_type=jnp.float32) + jnp.dot(
        factors, inv_low, preferred_element_type=jnp.float32
    )
    proj_high, proj_low = halves(proj)
    proj_ref[:, :k] = proj_high
    proj_ref[:, k:] = proj_low

    def low_wait(i):
        g_, h = i // nh, i % nh
        pan_copy(0, g_ * np_ + h * nl + lax.rem(lo + 1, nl), me).wait_recv()

    loop(0, n_low, low_wait)

    near.wait()
    loop(1, nb, lambda j: rs_copy(j).wait_send())
    loop(1, ns, lambda i: x_copy(i).wait_send())
    loop(1, nb, lambda j: gram_copy(j).wait_send())
    loop(1, total, lambda j: sum_copy(j).wait_send())
    loop(1, ng, lambda i: gene_send(i).wait_send())
    loop(0, n_high, lambda i: high_send(i).wait_send())
    loop(0, n_low, lambda i: low_send(i).wait_send())


def assoc_kernel(norm_scale, panel_ref, proj_ref, fac_ref, dosage_ref, out_ref):
    panel = panel_ref[...]
    k = fac_ref.shape[1]
    both = jnp.dot(panel, proj_ref[...], preferred_element_type=jnp.float32)
    coef = (both[:, :k] + both[:, k:]).astype(jnp.bfloat16)
    fitted = lax.dot_general(
        coef, fac_ref[...], (((1,), (1,)), ((), ())), preferred_element_type=jnp.float32
    )
    residual = (panel.astype(jnp.float32) - fitted).astype(jnp.bfloat16)
    totals = jnp.dot(residual, dosage_ref[...], preferred_element_type=jnp.float32)
    out_ref[...] = (totals * norm_scale).astype(jnp.bfloat16)


def body(expression, loadings, dosage):
    ns, ng, np_ = lax.axis_size("samp"), lax.axis_size("gene"), lax.axis_size("snp")
    nb = ng * np_
    total = ns * nb
    s_loc, g_loc = expression.shape
    k = loadings.shape[1]
    gp = g_loc // ns
    samples, snps = dosage.shape
    rows_f, rows_g = s_loc // nb, k // nb
    f32, bf16 = jnp.float32, jnp.bfloat16
    dma = pltpu.SemaphoreType.DMA
    vmem = pl.BlockSpec(memory_space=pltpu.VMEM)
    n_pan = ng + np_ * ng + nb
    limit_exchange = 8 * MIB + 4 * (nb * gp * samples + samples * k + 2 * g_loc * s_loc + samples * snps)
    limit_assoc = 8 * MIB + 6 * (samples * snps + 1024 * samples)
    panels, factors, proj, near = pl.pallas_call(
        functools.partial(factor_kernel, (ns, ng, np_)),
        out_shape=(
            jax.ShapeDtypeStruct((nb, gp, samples), bf16),
            jax.ShapeDtypeStruct((samples, k), bf16),
            jax.ShapeDtypeStruct((samples, 2 * k), bf16),
            jax.ShapeDtypeStruct((samples, snps), bf16),
        ),
        in_specs=[pl.BlockSpec(memory_space=pltpu.HBM)] * 3,
        out_specs=(vmem, vmem, vmem, vmem),
        scratch_shapes=[
            pltpu.VMEM((nb, rows_f + rows_g, k), f32),
            pltpu.VMEM((nb, rows_f + rows_g, k), f32),
            pltpu.VMEM((rows_f + rows_g, k), f32),
            pltpu.VMEM((k, k), f32),
            pltpu.VMEM((samples, k), f32),
            pltpu.VMEM((g_loc, s_loc), bf16),
            pltpu.VMEM((s_loc, g_loc), bf16),
            pltpu.VMEM((g_loc, k), bf16),
            dma((nb,)), dma((nb,)), dma((total,)), dma((total,)), dma((nb,)), dma((nb,)),
            dma((ns,)), dma((ns,)), dma((n_pan,)), dma((nb,)), dma, dma((2,)),
        ],
        compiler_params=pltpu.CompilerParams(
            collective_id=0, has_side_effects=True, vmem_limit_bytes=limit_exchange
        ),
        cost_estimate=pl.CostEstimate(
            flops=8 * samples * k * (g_loc + k), bytes_accessed=64 * nb * gp * samples, transcendentals=0
        ),
        name="factor_exchange",
    )(expression, loadings, dosage)
    rows = min(4 * gp, nb * gp)
    const = lambda i: (0, 0)
    out = pl.pallas_call(
        functools.partial(assoc_kernel, 1.0 / samples**0.5),
        grid=(nb * gp // rows,),
        out_shape=jax.ShapeDtypeStruct((nb * gp, snps), bf16),
        in_specs=[
            pl.BlockSpec((rows, samples), lambda i: (i, 0)),
            pl.BlockSpec((samples, 2 * k), const),
            pl.BlockSpec((samples, k), const),
            pl.BlockSpec((samples, snps), const),
        ],
        out_specs=pl.BlockSpec((rows, snps), lambda i: (i, 0)),
        compiler_params=pltpu.CompilerParams(vmem_limit_bytes=limit_assoc),
        cost_estimate=pl.CostEstimate(
            flops=2 * nb * gp * samples * (snps + 3 * k),
            bytes_accessed=2 * (nb * gp * (samples + snps) + samples * snps),
            transcendentals=0,
        ),
        name="association",
    )(panels.reshape(nb * gp, samples), proj, factors, near)
    return out.reshape(nb, 1, gp, snps)


def solution(mesh):
    placed = (P("samp", ("gene", "snp")), P(("gene", "snp"), None), P(None, ("gene", "snp")))
    return jax.shard_map(
        body,
        mesh=mesh,
        in_specs=placed,
        out_specs=P(None, "samp", None, ("gene", "snp")),
        check_vma=False,
    )
```

```python
import functools

import jax
import jax.numpy as jnp
from jax import lax
from jax.experimental import pallas as pl
from jax.experimental.pallas import tpu as pltpu
from jax.sharding import PartitionSpec as P

ridge_factor = 1.0
ridge_sample = 1.0
MESH = pl.DeviceIdType.MESH
MIB = 1024 * 1024


def eye(n, value):
    rows = lax.broadcasted_iota(jnp.int32, (n, n), 0)
    cols = lax.broadcasted_iota(jnp.int32, (n, n), 1)
    return jnp.where(rows == cols, jnp.float32(value), jnp.float32(0.0))


def reciprocal(d):
    guess = pltpu.reciprocal(d, approx=True)
    return guess * (2.0 - d * guess)


def sweep_block(rows, i):
    n = rows[0].shape[1]
    at = 8 * i
    lane = lax.broadcasted_iota(jnp.int32, (8, n), 1)
    sub = lax.broadcasted_iota(jnp.int32, (8, n), 0)

    def full(x):
        return jnp.broadcast_to(x, (8, n))

    top = rows[i]
    cols = [full(top[:, at + j : at + j + 1]) for j in range(8)]
    for k in range(8):
        on = sub == k
        col = cols[k]
        inv = reciprocal(full(col[k : k + 1]))
        top = jnp.where(lane == at + k, jnp.where(on, 1.0, 0.0), top)
        pivot_row = full(top[k : k + 1]) * inv
        top = jnp.where(on, pivot_row, top - col * pivot_row)
        for j in range(k + 1, 8):
            pivot_col = full(cols[j][k : k + 1]) * inv
            cols[j] = jnp.where(on, pivot_col, cols[j] - col * pivot_col)
    weights = [full(top[j : j + 1]) for j in range(8)]
    in_block = (lane >= at) & (lane < at + 8)
    out = []
    for r, x in enumerate(rows):
        if r == i:
            out.append(top)
            continue
        even = full(x[:, at : at + 1]) * weights[0]
        odd = full(x[:, at + 1 : at + 2]) * weights[1]
        for j in range(2, 8, 2):
            even = even + full(x[:, at + j : at + j + 1]) * weights[j]
            odd = odd + full(x[:, at + j + 1 : at + j + 2]) * weights[j + 1]
        out.append(jnp.where(in_block, 0.0, x) - (even + odd))
    return out


def spd_inverse(a, midway=None, at=0):
    n = a.shape[0]
    rows = [a[8 * i : 8 * i + 8] for i in range(n // 8)]
    for i in range(n // 8):
        if midway is not None and i == at:
            midway()
        rows = sweep_block(rows, i)
    return jnp.concatenate(rows, axis=0)


def halves(x):
    high = x.astype(jnp.bfloat16)
    low = (x - high.astype(jnp.float32)).astype(jnp.bfloat16)
    return high, low


def factor_kernel(
    sizes, expr_ref, load_ref, dosage_ref, panel_ref, fac_ref, proj_ref, near_ref,
    part, got, own, gram_all, sum_all, expr_t, expr_in, load_in,
    rs_send, rs_recv, ag_send, ag_recv, gram_send, gram_recv, sh_send, sh_recv, x_send, x_recv, pan_send, pan_recv, near_sem, in_sem,
):
    ns, ng, np_ = sizes
    nb = ng * np_
    nl = 2 if np_ % 2 == 0 else 1
    nh = np_ // nl
    s_loc = expr_ref.shape[0]
    k = load_ref.shape[1]
    gp = expr_ref.shape[1] // ns
    rows_f, rows_g = s_loc // nb, k // nb
    s, g, p = lax.axis_index("samp"), lax.axis_index("gene"), lax.axis_index("snp")
    b = g * np_ + p
    hi, lo = p // nl, p % nl

    staged = (
        pltpu.make_async_copy(expr_ref, expr_in, in_sem.at[0]),
        pltpu.make_async_copy(load_ref, load_in, in_sem.at[1]),
    )
    for copy in staged:
        copy.start()
    barrier = pltpu.get_barrier_semaphore()

    for j in range(1, nb):
        peer = lax.rem(b + j, nb)
        pl.semaphore_signal(
            barrier, inc=1, device_id=(s, peer // np_, peer % np_), device_id_type=MESH
        )
    for i in range(1, ns):
        pl.semaphore_signal(
            barrier, inc=1, device_id=(lax.rem(s + i, ns), g, p), device_id_type=MESH
        )

    near = pltpu.make_async_copy(dosage_ref, near_ref, near_sem)
    near.start()
    for copy in staged:
        copy.wait()
    expr = expr_in[...]
    load = load_in[...]
    fac_part = jnp.dot(expr, load, preferred_element_type=jnp.float32)
    part[:, :rows_f, :] = fac_part.reshape(nb, rows_f, k)
    gram_part = lax.dot_general(load, load, (((0,), (0,)), ((), ())), preferred_element_type=jnp.float32)
    part[:, rows_f:, :] = gram_part.reshape(nb, rows_g, k)
    expr_t[...] = expr.T

    pl.semaphore_wait(barrier, nb + ns - 2)

    def rs_copy(j):
        peer = lax.rem(b + j, nb)
        return pltpu.make_async_remote_copy(
            src_ref=part.at[peer], dst_ref=got.at[j],
            send_sem=rs_send.at[j], recv_sem=rs_recv.at[j],
            device_id=(s, peer // np_, peer % np_), device_id_type=MESH,
        )

    def x_copy(i, arriving=False):
        peer = lax.rem(s + i, ns)
        source = lax.rem(s - i + ns, ns) if arriving else s
        return pltpu.make_async_remote_copy(
            src_ref=expr_t.at[pl.ds(pl.multiple_of(peer * gp, gp), gp), :],
            dst_ref=panel_ref.at[b, :, pl.ds(pl.multiple_of(source * s_loc, s_loc), s_loc)],
            send_sem=x_send.at[i], recv_sem=x_recv.at[i],
            device_id=(peer, g, p), device_id_type=MESH,
        )

    def loop(lo_, hi_, fn):
        for i in range(lo_, hi_):
            fn(i)

    loop(1, nb, lambda j: rs_copy(j).start())
    loop(1, ns, lambda i: x_copy(i).start())
    panel_ref[b, :, pl.ds(pl.multiple_of(s * s_loc, s_loc), s_loc)] = expr_t[
        pl.ds(pl.multiple_of(s * gp, gp), gp), :
    ]

    def pan_copy(slot, block, dev):
        return pltpu.make_async_remote_copy(
            src_ref=panel_ref.at[block], dst_ref=panel_ref.at[block],
            send_sem=pan_send.at[slot], recv_sem=pan_recv.at[block],
            device_id=dev, device_id_type=MESH,
        )

    def gene_send(i):
        return pan_copy(i, b, (s, lax.rem(g + i, ng), p))

    def high_send(i):
        h, g_ = 1 + i % (nh - 1), lax.rem(g + i // (nh - 1), ng)
        return pan_copy(ng + i, g_ * np_ + p, (s, g, lax.rem(hi + h, nh) * nl + lo))

    def low_send(i):
        g_, h = i // nh, i % nh
        return pan_copy(
            ng + ng * (nh - 1) + i, g_ * np_ + h * nl + lo, (s, g, hi * nl + lax.rem(lo + 1, nl))
        )

    n_high = ng * (nh - 1)
    n_low = nb // nl if nl > 1 else 0

    loop(1, ns, lambda i: x_copy(i, True).wait_recv())
    loop(1, ng, lambda i: gene_send(i).start())
    loop(0, nh - 1, lambda i: high_send(i).start())

    loop(1, nb, lambda j: rs_copy(j).wait_recv())
    acc = part[b]
    for j in range(1, nb):
        acc = acc + got[j]
    own[...] = acc

    def gram_copy(j, arriving=False):
        peer = lax.rem(b + j, nb)
        source = lax.rem(b - j + nb, nb) if arriving else b
        return pltpu.make_async_remote_copy(
            src_ref=own.at[pl.ds(rows_f, rows_g), :],
            dst_ref=gram_all.at[pl.ds(pl.multiple_of(source * rows_g, rows_g), rows_g), :],
            send_sem=gram_send.at[j], recv_sem=gram_recv.at[j],
            device_id=(s, peer // np_, peer % np_), device_id_type=MESH,
        )

    def sum_copy(j, arriving=False):
        peer = lax.rem(b + j, nb)
        source = lax.rem(b - j + nb, nb) if arriving else b
        return pltpu.make_async_remote_copy(
            src_ref=own.at[pl.ds(0, rows_f), :],
            dst_ref=sum_all.at[s, pl.ds(pl.multiple_of(source * rows_f, rows_f), rows_f), :],
            send_sem=ag_send.at[j], recv_sem=ag_recv.at[j],
            device_id=(s, peer // np_, peer % np_), device_id_type=MESH,
        )

    def shard_copy(i, arriving=False):
        source = lax.rem(s - i + ns, ns) if arriving else s
        return pltpu.make_async_remote_copy(
            src_ref=sum_all.at[s], dst_ref=sum_all.at[source],
            send_sem=sh_send.at[i], recv_sem=sh_recv.at[i],
            device_id=(lax.rem(s + i, ns), g, p), device_id_type=MESH,
        )

    loop(1, nb, lambda j: gram_copy(j).start())
    loop(1, nb, lambda j: sum_copy(j).start())
    gram_all[pl.ds(pl.multiple_of(b * rows_g, rows_g), rows_g), :] = acc[rows_f:]
    sum_all[s, pl.ds(pl.multiple_of(b * rows_f, rows_f), rows_f), :] = acc[:rows_f]


    loop(1, nb, lambda j: gram_copy(j, True).wait_recv())
    me = (s, g, p)

    def spread_sums():
        loop(1, nb, lambda j: sum_copy(j, True).wait_recv())
        loop(1, ns, lambda i: shard_copy(i).start())

    gram_inv = spd_inverse(gram_all[...] + eye(k, ridge_factor), spread_sums, k // 32)
    loop(1, ng, lambda i: pan_copy(0, lax.rem(g + i, ng) * np_ + p, me).wait_recv())
    loop(nh - 1, n_high, lambda i: high_send(i).start())

    loop(1, ns, lambda i: shard_copy(i, True).wait_recv())
    factors = jnp.dot(
        sum_all[...].reshape(ns * s_loc, k), gram_inv, preferred_element_type=jnp.float32, precision=lax.Precision.HIGHEST
    ).astype(jnp.bfloat16)
    fac_ref[...] = factors
    hess = lax.dot_general(
        factors, factors, (((0,), (0,)), ((), ())), preferred_element_type=jnp.float32
    )

    def high_wait(i):
        h, g_ = 1 + i // ng, i % ng
        pan_copy(0, g_ * np_ + lax.rem(hi + h, nh) * nl + lo, me).wait_recv()

    def spread_panels():
        loop(0, n_high, high_wait)
        loop(0, n_low, lambda i: low_send(i).start())

    hess_inv = spd_inverse(hess + eye(k, ridge_sample), spread_panels, 3 * k // 32)
    inv_high, inv_low = halves(hess_inv)
    proj = jnp.dot(factors, inv_high, preferred_element_type=jnp.float32) + jnp.dot(
        factors, inv_low, preferred_element_type=jnp.float32
    )
    proj_high, proj_low = halves(proj)
    proj_ref[:, :k] = proj_high
    proj_ref[:, k:] = proj_low

    def low_wait(i):
        g_, h = i // nh, i % nh
        pan_copy(0, g_ * np_ + h * nl + lax.rem(lo + 1, nl), me).wait_recv()

    loop(0, n_low, low_wait)

    near.wait()
    loop(1, nb, lambda j: rs_copy(j).wait_send())
    loop(1, ns, lambda i: x_copy(i).wait_send())
    loop(1, nb, lambda j: gram_copy(j).wait_send())
    loop(1, nb, lambda j: sum_copy(j).wait_send())
    loop(1, ns, lambda i: shard_copy(i).wait_send())
    loop(1, ng, lambda i: gene_send(i).wait_send())
    loop(0, n_high, lambda i: high_send(i).wait_send())
    loop(0, n_low, lambda i: low_send(i).wait_send())


def assoc_kernel(norm_scale, panel_ref, proj_ref, fac_ref, dosage_ref, out_ref):
    panel = panel_ref[...]
    k = fac_ref.shape[1]
    both = jnp.dot(panel, proj_ref[...], preferred_element_type=jnp.float32)
    coef = (both[:, :k] + both[:, k:]).astype(jnp.bfloat16)
    fitted = lax.dot_general(
        coef, fac_ref[...], (((1,), (1,)), ((), ())), preferred_element_type=jnp.float32
    )
    residual = (panel.astype(jnp.float32) - fitted).astype(jnp.bfloat16)
    totals = jnp.dot(residual, dosage_ref[...], preferred_element_type=jnp.float32)
    out_ref[...] = (totals * norm_scale).astype(jnp.bfloat16)


def body(expression, loadings, dosage):
    ns, ng, np_ = lax.axis_size("samp"), lax.axis_size("gene"), lax.axis_size("snp")
    nb = ng * np_
    s_loc, g_loc = expression.shape
    k = loadings.shape[1]
    gp = g_loc // ns
    samples, snps = dosage.shape
    rows_f, rows_g = s_loc // nb, k // nb
    f32, bf16 = jnp.float32, jnp.bfloat16
    dma = pltpu.SemaphoreType.DMA
    vmem = pl.BlockSpec(memory_space=pltpu.VMEM)
    n_pan = ng + np_ * ng + nb
    limit_exchange = 8 * MIB + 4 * (nb * gp * samples + samples * k + 2 * g_loc * s_loc + samples * snps)
    limit_assoc = 8 * MIB + 6 * (samples * snps + 1024 * samples)
    panels, factors, proj, near = pl.pallas_call(
        functools.partial(factor_kernel, (ns, ng, np_)),
        out_shape=(
            jax.ShapeDtypeStruct((nb, gp, samples), bf16),
            jax.ShapeDtypeStruct((samples, k), bf16),
            jax.ShapeDtypeStruct((samples, 2 * k), bf16),
            jax.ShapeDtypeStruct((samples, snps), bf16),
        ),
        in_specs=[pl.BlockSpec(memory_space=pltpu.HBM)] * 3,
        out_specs=(vmem, vmem, vmem, vmem),
        scratch_shapes=[
            pltpu.VMEM((nb, rows_f + rows_g, k), f32),
            pltpu.VMEM((nb, rows_f + rows_g, k), f32),
            pltpu.VMEM((rows_f + rows_g, k), f32),
            pltpu.VMEM((k, k), f32),
            pltpu.VMEM((ns, s_loc, k), f32),
            pltpu.VMEM((g_loc, s_loc), bf16),
            pltpu.VMEM((s_loc, g_loc), bf16),
            pltpu.VMEM((g_loc, k), bf16),
            dma((nb,)), dma((nb,)), dma((nb,)), dma((nb,)), dma((nb,)), dma((nb,)),
            dma((ns,)), dma((ns,)),
            dma((ns,)), dma((ns,)), dma((n_pan,)), dma((nb,)), dma, dma((2,)),
        ],
        compiler_params=pltpu.CompilerParams(
            collective_id=0, has_side_effects=True, vmem_limit_bytes=limit_exchange
        ),
        cost_estimate=pl.CostEstimate(
            flops=8 * samples * k * (g_loc + k), bytes_accessed=64 * nb * gp * samples, transcendentals=0
        ),
        name="factor_exchange",
    )(expression, loadings, dosage)
    rows = min(4 * gp, nb * gp)
    const = lambda i: (0, 0)
    out = pl.pallas_call(
        functools.partial(assoc_kernel, 1.0 / samples**0.5),
        grid=(nb * gp // rows,),
        out_shape=jax.ShapeDtypeStruct((nb * gp, snps), bf16),
        in_specs=[
            pl.BlockSpec((rows, samples), lambda i: (i, 0)),
            pl.BlockSpec((samples, 2 * k), const),
            pl.BlockSpec((samples, k), const),
            pl.BlockSpec((samples, snps), const),
        ],
        out_specs=pl.BlockSpec((rows, snps), lambda i: (i, 0)),
        compiler_params=pltpu.CompilerParams(vmem_limit_bytes=limit_assoc),
        cost_estimate=pl.CostEstimate(
            flops=2 * nb * gp * samples * (snps + 3 * k),
            bytes_accessed=2 * (nb * gp * (samples + snps) + samples * snps),
            transcendentals=0,
        ),
        name="association",
    )(panels.reshape(nb * gp, samples), proj, factors, near)
    return out.reshape(nb, 1, gp, snps)


def solution(mesh):
    placed = (P("samp", ("gene", "snp")), P(("gene", "snp"), None), P(None, ("gene", "snp")))
    return jax.shard_map(
        body,
        mesh=mesh,
        in_specs=placed,
        out_specs=P(None, "samp", None, ("gene", "snp")),
        check_vma=False,
    )
```
